512 devices in a mesh: seq: 64 (over y, z), tp: 8 (over x, core).
Axes of the slice: x: 4, y: 4, z: 16, core: 2. Of those that a mesh axis runs over, the one named last changes fastest.
Arguments:
- queries: bfloat16 [4096, 8192], P('seq', 'tp'), may hold values from -8 to 8
- keys: bfloat16 [4096, 1024], P('seq', 'tp'), may hold values from -8 to 8
- values: bfloat16 [4096, 1024], P('seq', 'tp'), may hold values from -6 to 6
- segment_ids: int32 [4096], P('seq'), may hold values from 0 to 17, as said below
- out_weight: bfloat16 [8192, 16384], P('tp', 'seq'), may hold values from -0.0625 to 0.0625
Outputs:
- mixed: bfloat16 [4096, 16384], P('tp', 'seq')
The draws below stay inside these ranges and needn't reach their ends.
Inputs may be any that keep to these rules, and one draw needn't show every extreme that they name: `segment_ids`: document ids start at 0 at the first token, never fall, and rise by at most one from a token to the next; one document covers exactly 2112 tokens.
All inputs are finite; a program needn't handle non-finite values.
Results may differ from the reference program's by a relative error of at most 0.019.
Values may be sent and summed in bfloat16 or wider, within the bound.
No kernel may reach another device: no remote copies, remote signals or barrier semaphores. Data moves between devices by JAX's collectives and lax.ppermute only.
A program may use at most 64 MiB of HBM per device.

```python
import math
import jax
import jax.numpy as jnp
from jax import lax

TOK_DEV = 64
HD = 128
KVH = 8
GROUP = 8
D = 16384
TOKENS = 4096


def doc_segments(key):
    key = jax.random.fold_in(key, 11)
    order_key, begin_key = jax.random.split(key)
    token_index = jnp.arange(TOKENS, dtype=jnp.int32)
    long_length = TOKENS // 2 + TOK_DEV
    long_start = jax.random.randint(begin_key, (), 1, TOKENS - long_length)
    long_end = long_start + long_length
    extra_count = max(1, (TOKENS // 2 - TOK_DEV) // 128)
    ranking = jax.random.permutation(order_key, TOKENS).astype(jnp.int32)
    blocked = (token_index >= long_start) & (token_index <= long_end) | (token_index == 0)
    ranking = jnp.where(blocked, -1, ranking)
    picked_values, picked_index = lax.top_k(ranking, extra_count)
    extra_flags = jnp.zeros((TOKENS,), jnp.int32).at[picked_index].set(1)
    start_flags = (extra_flags == 1) | (token_index == long_start) | (token_index == long_end) | (token_index == 0)
    return jnp.cumsum(start_flags.astype(jnp.int32)) - 1


def draw_segment_ids(key, part):
    return doc_segments(key)


def draw_queries(key, part):
    key = jax.random.fold_in(key, 3)
    full_shape = (TOKENS, KVH, GROUP, HD)
    base_draw = jnp.clip(jax.random.normal(key, full_shape), -6.0, 6.0)
    return base_draw.reshape(TOKENS, KVH * GROUP * HD).astype(jnp.bfloat16)


def draw_keys(key, part):
    key = jax.random.fold_in(key, 5)
    full_shape = (TOKENS, KVH, HD)
    base_draw = jnp.clip(jax.random.normal(key, full_shape), -6.0, 6.0)
    return base_draw.reshape(TOKENS, KVH * HD).astype(jnp.bfloat16)


def level_of(stream_key, shape, shards, smallest, largest):
    gain = 1.0
    for axis_at, shards_of in shards:
        heights = jax.random.uniform(jax.random.fold_in(jax.random.fold_in(stream_key, 6), axis_at), (shards_of,), jnp.float32, smallest / len(shards), largest / len(shards))
        gain = gain * jnp.repeat(jnp.exp(heights), shape[axis_at] // shards_of).reshape((-1,) + (1,) * (len(shape) - 1 - axis_at))
    return gain


def bell_draw(stream_key, dims, spread, most, cuts=(), held_as=jnp.bfloat16):
    factor_of = level_of(stream_key, dims, cuts, -0.22, 0.18) if cuts else 1.0
    values = jax.random.normal(stream_key, dims, jnp.float32) * spread * factor_of
    return jnp.minimum(jnp.maximum(values, -most), most).astype(held_as)


def setup_inputs(seed: int = 0) -> dict:
    arg_keys = jax.random.split(jax.random.key(seed), 6)
    queries = draw_queries(jax.random.fold_in(arg_keys[5], 71), 0)
    keys = draw_keys(jax.random.fold_in(arg_keys[5], 71), 0)
    values = bell_draw(arg_keys[2], (TOKENS, KVH * HD), 1.0, 6.0, ((0, 64), (1, 8)))
    segment_ids = draw_segment_ids(jax.random.fold_in(arg_keys[5], 71), 0)
    out_weight = bell_draw(arg_keys[4], (KVH * GROUP * HD, D), (KVH * GROUP * HD) ** -0.5, 0.0625, ((0, 8), (1, 64)))
    return dict(queries=queries, keys=keys, values=values, segment_ids=segment_ids, out_weight=out_weight)


masked_score = -1e+30

def reference(queries, keys, values, segment_ids, out_weight):
    score_scale = 1.0 / math.sqrt(HD)
    query_heads = queries.reshape(TOKENS, KVH, GROUP, HD).astype(jnp.float32)
    key_heads = keys.reshape(TOKENS, KVH, HD).astype(jnp.float32)
    value_heads = values.reshape(TOKENS, KVH, HD).astype(jnp.float32)
    key_pos = jnp.arange(TOKENS, dtype=jnp.int32)

    def query_block(first_row):
        block_rows = lax.dynamic_slice_in_dim(query_heads, first_row, TOK_DEV, 0)
        query_pos = first_row + jnp.arange(TOK_DEV, dtype=jnp.int32)
        query_seg = lax.dynamic_slice_in_dim(segment_ids, first_row, TOK_DEV, 0)
        allowed = (key_pos[None, :] <= query_pos[:, None]) & (segment_ids[None, :] == query_seg[:, None])
        keep_mask = allowed[:, None, None, :]
        scores = jnp.einsum('tkgd,skd->tkgs', block_rows, key_heads, precision=lax.Precision.HIGHEST) * score_scale
        row_max = lax.optimization_barrier(jnp.max(jnp.where(keep_mask, scores, masked_score), axis=-1))
        weights = jnp.where(keep_mask, jnp.exp(scores - row_max[..., None]), 0.0)
        row_sum = lax.optimization_barrier(jnp.sum(weights, axis=-1))
        rounded = lax.optimization_barrier(weights.astype(jnp.bfloat16)).astype(jnp.float32)
        combined = jnp.einsum('tkgs,skd->tkgd', rounded, value_heads, precision=lax.Precision.HIGHEST)
        return (combined / row_sum[..., None]).astype(jnp.bfloat16).reshape(TOK_DEV, KVH * GROUP * HD)
    starts = jnp.arange(TOKENS // TOK_DEV, dtype=jnp.int32) * TOK_DEV
    attended = lax.map(query_block, starts).reshape(TOKENS, KVH * GROUP * HD)
    return jnp.dot(attended, out_weight, preferred_element_type=jnp.float32).astype(jnp.bfloat16)
```

```python
import math

import jax
import jax.numpy as jnp
from jax import lax
from jax.experimental import pallas as pl
from jax.experimental.pallas import tpu as pltpu
from jax.sharding import PartitionSpec as P

HD = 128
GROUP = 8
TOK = 64
NY, NZ, NX, NC = 4, 16, 4, 2
CHUNK = 4 * TOK
CHUNKS = 10
SEG_ROWS = 16
BAND = NZ * TOK + SEG_ROWS
MASKED = -1e30

Y_GROUPS = [[y * NZ + z for y in range(NY)] for z in range(NZ)]
Z_GROUPS = [[y * NZ + z for z in range(NZ)] for y in range(NY)]
X_GROUPS = [[x * NC + c for x in range(NX)] for c in range(NC)]
CORE_SWAP = [(t, t ^ 1) for t in range(NX * NC)]


def flat(y, z, x, c):
    return ((y * NZ + z) * NX + x) * NC + c


XY_SWAP = [
    (flat(y, z, x, c), flat(x, z, y, c))
    for y in range(NY)
    for z in range(NZ)
    for x in range(NX)
    for c in range(NC)
]


def attend(q_ref, seg_ref, kv_ref, ids_ref, out_ref, score_ref):
    rank = lax.axis_index("seq")
    first_chunk = jnp.maximum(rank // 4 - (CHUNKS - 1), 0)
    own = seg_ref[...].astype(jnp.float32)
    rows = lax.broadcasted_iota(jnp.int32, (TOK, TOK), 0)
    cols = lax.broadcasted_iota(jnp.int32, (TOK, TOK), 1)
    across = jnp.broadcast_to(own, (TOK, TOK))
    down = jnp.sum(jnp.where(rows == cols, across, 0.0), axis=1, keepdims=True)
    below = jnp.sum((across < down).astype(jnp.float32), axis=1, keepdims=True)
    head_id = jnp.min(down)
    pairs = ids_ref[...].astype(jnp.float32)
    ids = pairs[:, :TOK] + 128.0 * pairs[:, TOK:]
    block = lax.broadcasted_iota(jnp.int32, ids.shape, 0)
    earlier = jnp.sum(((ids == head_id) & (block < rank)).astype(jnp.float32))
    begin = (rank * TOK).astype(jnp.float32) + jnp.where(down == head_id, -earlier, below)
    begin = begin.astype(jnp.int32)
    position = rank * TOK + lax.broadcasted_iota(jnp.int32, (TOK, 1), 0)

    queries = jnp.concatenate([q_ref[:, g * HD : (g + 1) * HD] for g in range(GROUP)], axis=0)
    best = jnp.full((GROUP * TOK, HD), MASKED, jnp.float32)

    def key_rows(i):
        chunk = first_chunk + i
        return pl.ds(pl.multiple_of(chunk // 4 * BAND + chunk % 4 * CHUNK, 16), CHUNK)

    for i in range(CHUNKS):
        keys = kv_ref[key_rows(i), :HD]
        scores = lax.dot_general(
            queries, keys, (((1,), (1,)), ((), ())), preferred_element_type=jnp.float32
        )
        at = (first_chunk + i) * CHUNK + lax.broadcasted_iota(jnp.int32, (TOK, CHUNK), 1)
        keep = (at >= begin) & (at <= position)
        scores = jnp.where(keep[None], scores.reshape(GROUP, TOK, CHUNK), MASKED)
        scores = scores.reshape(GROUP * TOK, CHUNK)
        score_ref[i] = scores
        best = jnp.maximum(best, jnp.maximum(scores[:, :HD], scores[:, HD:]))
    scale = math.log2(math.e) / math.sqrt(HD)
    top = jnp.max(best, axis=1, keepdims=True) * scale
    total = jnp.zeros((GROUP * TOK, HD), jnp.float32)
    mixed = jnp.zeros((GROUP * TOK, HD), jnp.float32)
    for i in range(CHUNKS):
        weights = jnp.exp2(score_ref[i] * scale - top)
        total += weights[:, :HD] + weights[:, HD:]
        mixed += jnp.dot(
            weights.astype(jnp.bfloat16),
            kv_ref[key_rows(i), HD:],
            preferred_element_type=jnp.float32,
        )
    result = (mixed / jnp.sum(total, axis=1, keepdims=True)).astype(jnp.bfloat16)
    for g in range(GROUP):
        out_ref[:, g * HD : (g + 1) * HD] = result[g * TOK : (g + 1) * TOK]


def body(queries, keys, values, segment_ids, out_weight):
    core = lax.axis_index("tp") % NC
    weight = lax.all_gather(out_weight, "seq", axis_index_groups=Y_GROUPS)

    pair = jnp.concatenate([keys, values], axis=1)
    low, high = segment_ids % 128, segment_ids // 128
    tag = jnp.concatenate([low, high, jnp.zeros_like(low), jnp.zeros_like(low)])[None]
    tag = jnp.pad(tag, ((0, SEG_ROWS - 1), (0, 0))).astype(jnp.bfloat16)
    message = jnp.concatenate([pair, tag], axis=0)
    band = lax.all_gather(message, "seq", axis_index_groups=Z_GROUPS)
    band = jnp.concatenate([band[:, :TOK].reshape(NZ * TOK, 2 * HD), band[:, TOK]], axis=0)
    bands = lax.all_gather(
        band.astype(jnp.float16), "seq", axis_index_groups=Y_GROUPS, tiled=True
    ).astype(jnp.bfloat16)
    ids = bands.reshape(NY, BAND, 2 * HD)[:, NZ * TOK :, :HD].reshape(NY * NZ, HD)

    attended = pl.pallas_call(
        attend,
        out_shape=jax.ShapeDtypeStruct((TOK, GROUP * HD), jnp.bfloat16),
        in_specs=[pl.BlockSpec(memory_space=pltpu.VMEM)] * 4,
        out_specs=pl.BlockSpec(memory_space=pltpu.VMEM),
        scratch_shapes=[pltpu.VMEM((CHUNKS, GROUP * TOK, CHUNK), jnp.float32)],
        compiler_params=pltpu.CompilerParams(vmem_limit_bytes=40 * 1024 * 1024),
        cost_estimate=pl.CostEstimate(
            flops=4 * GROUP * TOK * CHUNKS * CHUNK * HD,
            bytes_accessed=3 * 1024 * 1024,
            transcendentals=GROUP * TOK * CHUNKS * CHUNK,
        ),
    )(queries, segment_ids.reshape(1, TOK), bands, ids)

    rows = lax.all_gather(attended.astype(jnp.float16), "seq", axis_index_groups=Z_GROUPS)
    rows = rows.astype(jnp.bfloat16).reshape(NC, NZ * TOK // NC, GROUP * HD)

    def project(which):
        half = lax.dynamic_index_in_dim(rows, which, 0, keepdims=False)
        return jnp.einsum("rk,ykn->yrn", half, weight, preferred_element_type=jnp.float32)

    theirs = lax.ppermute(project(1 - core).astype(jnp.bfloat16), "tp", CORE_SWAP)
    both = (project(core) + theirs.astype(jnp.float32)).astype(jnp.bfloat16)
    parts = lax.all_to_all(both, "tp", 0, 0, axis_index_groups=X_GROUPS, tiled=True)
    mixed = jnp.sum(parts.astype(jnp.float32), axis=0).astype(jnp.bfloat16)
    return lax.ppermute(mixed, ("seq", "tp"), XY_SWAP)


def solution(mesh):
    return jax.shard_map(
        body,
        mesh=mesh,
        in_specs=(P("seq", "tp"), P("seq", "tp"), P("seq", "tp"), P("seq"), P("tp", "seq")),
        out_specs=P("tp", "seq"),
        check_vma=False,
    )
```

```python
import functools
import math

import jax
import jax.numpy as jnp
from jax import lax
from jax.experimental import pallas as pl
from jax.experimental.pallas import tpu as pltpu
from jax.sharding import PartitionSpec as P

HD = 128
GROUP = 8
TOK = 64
NY, NZ, NX, NC = 4, 16, 4, 2
CHUNK = 4 * TOK
CHUNKS = 10
PLANE = NZ * TOK
SEG_ROWS = 16
BAND = 2 * PLANE + SEG_ROWS
MASKED = -1e30
VMEM = pl.BlockSpec(memory_space=pltpu.VMEM)

Y_GROUPS = [[y * NZ + z for y in range(NY)] for z in range(NZ)]
Z_GROUPS = [[y * NZ + z for z in range(NZ)] for y in range(NY)]
CORE_SWAP = [(t, t ^ 1) for t in range(NX * NC)]


def flat(y, z, x, c):
    return ((y * NZ + z) * NX + x) * NC + c


PLANE_GROUPS = [
    [flat(y, z, x, c) for y in range(NY) for x in range(NX)] for z in range(NZ) for c in range(NC)
]
QUERY_MOVE = [(y * NZ + z, (y - z) % NY * NZ + z) for y in range(NY) for z in range(NZ)]


def y_flip(d):
    return [(y * NZ + z, (y ^ d) * NZ + z) for y in range(NY) for z in range(NZ)]


def attend(q_ref, kv_ref, ids_ref, out_ref, score_ref):
    at_y, at_z = lax.axis_index("seq") // NZ, lax.axis_index("seq") % NZ
    rank = (at_y + at_z) % NY * NZ + at_z
    first_chunk = jnp.maximum(rank // 4 - (CHUNKS - 1), 0)
    pairs = ids_ref[...]
    ids = pairs[:, :TOK] + 128.0 * pairs[:, TOK:]
    own = ids_ref[pl.ds(rank, 1), :]
    own = own[:, :TOK] + 128.0 * own[:, TOK:]
    rows = lax.broadcasted_iota(jnp.int32, (TOK, TOK), 0)
    cols = lax.broadcasted_iota(jnp.int32, (TOK, TOK), 1)
    across = jnp.broadcast_to(own, (TOK, TOK))
    down = jnp.sum(jnp.where(rows == cols, across, 0.0), axis=1, keepdims=True)
    below = jnp.sum((across < down).astype(jnp.float32), axis=1, keepdims=True)
    head_id = jnp.min(own, axis=1, keepdims=True)
    earlier = jnp.sum(((ids == head_id) & (rows < rank)).astype(jnp.float32))
    begin = (rank * TOK).astype(jnp.float32) + jnp.where(down == head_id, -earlier, below)
    begin = begin.astype(jnp.int32)
    position = rank * TOK + lax.broadcasted_iota(jnp.int32, (TOK, 1), 0)

    queries = jnp.concatenate([q_ref[:, g * HD : (g + 1) * HD] for g in range(GROUP)], axis=0)
    best = jnp.full((GROUP * TOK, HD), MASKED, jnp.float32)

    def rows_at(i, offset):
        chunk = first_chunk + i
        return pl.ds(pl.multiple_of(chunk // 4 * BAND + chunk % 4 * CHUNK + offset, 16), CHUNK)

    for i in range(CHUNKS):
        scores = lax.dot_general(
            queries,
            kv_ref[rows_at(i, 0), :],
            (((1,), (1,)), ((), ())),
            preferred_element_type=jnp.float32,
        )
        at = (first_chunk + i) * CHUNK + lax.broadcasted_iota(jnp.int32, (TOK, CHUNK), 1)
        keep = (at >= begin) & (at <= position)
        scores = jnp.where(keep[None], scores.reshape(GROUP, TOK, CHUNK), MASKED)
        scores = scores.reshape(GROUP * TOK, CHUNK)
        score_ref[i] = scores
        best = jnp.maximum(best, jnp.maximum(scores[:, :HD], scores[:, HD:]))
    scale = math.log2(math.e) / math.sqrt(HD)
    top = jnp.max(best, axis=1, keepdims=True) * scale
    total = jnp.zeros((GROUP * TOK, HD), jnp.float32)
    mixed = jnp.zeros((GROUP * TOK, HD), jnp.float32)
    for i in range(CHUNKS):
        weights = jnp.exp2(score_ref[i] * scale - top)
        total += weights[:, :HD] + weights[:, HD:]
        mixed += jnp.dot(
            weights.astype(jnp.bfloat16),
            kv_ref[rows_at(i, PLANE), :],
            preferred_element_type=jnp.float32,
        )
    result = (mixed / jnp.sum(total, axis=1, keepdims=True)).astype(jnp.bfloat16)
    for g in range(GROUP):
        out_ref[:, g * HD : (g + 1) * HD] = result[g * TOK : (g + 1) * TOK]


def project(own, rows_ref, weight_ref, *refs):
    out_ref, picked_ref = refs[-2:]
    at_y, core = lax.axis_index("seq") // NZ, lax.axis_index("tp") % NC
    half = core if own else 1 - core
    for x in range(NX):
        for j in range(2):
            block = (2 * half + j) * 4 + (x + NY - at_y) % NY
            source = pl.ds(pl.multiple_of(block * TOK, TOK), TOK)
            picked_ref[pl.ds((2 * x + j) * TOK, TOK), :] = rows_ref[source, :]
    for d in range(NY):
        part = jnp.dot(picked_ref[...], weight_ref[d], preferred_element_type=jnp.float32)
        width = part.shape[-1]
        part = part.reshape(NX, 2, TOK, width)
        spot = pl.ds(d * NX, NX)
        for j in range(2):
            across = slice(j * width, (j + 1) * width)
            half_part = part[:, j]
            if own:
                half_part += refs[0][spot, :, across].astype(jnp.float32)
            out_ref[spot, :, across] = half_part.astype(jnp.bfloat16)


def combine(parts_ref, out_ref):
    at_x = lax.axis_index("tp") // NC
    width = out_ref.shape[1]
    for y in range(NY):
        total = parts_ref[y * NX].astype(jnp.float32)
        for x in range(1, NX):
            total += parts_ref[y * NX + x].astype(jnp.float32)
        total = total.astype(jnp.bfloat16)
        for j in range(2):
            block = 4 * j + (at_x + NY - y) % NY
            spot = pl.ds(pl.multiple_of(block * TOK, TOK), TOK)
            out_ref[spot, :] = total[:, j * width : (j + 1) * width]


def body(queries, keys, values, segment_ids, out_weight):
    width = out_weight.shape[1]
    copies = jnp.broadcast_to(out_weight[None], (NY,) + out_weight.shape)
    weights = lax.all_to_all(copies, "seq", 0, 0, axis_index_groups=Y_GROUPS, tiled=True)
    queries = lax.ppermute(queries, "seq", QUERY_MOVE)

    tag = jnp.concatenate([segment_ids % 128, segment_ids // 128])[None]
    tag = jnp.pad(tag, ((0, SEG_ROWS - 1), (0, 0))).astype(jnp.bfloat16)
    message = jnp.concatenate([keys, values, tag], axis=0)
    plane = lax.all_gather(message, "seq", axis_index_groups=Z_GROUPS)
    plane = jnp.concatenate(
        [
            plane[:, :TOK].reshape(PLANE, HD),
            plane[:, TOK : 2 * TOK].reshape(PLANE, HD),
            plane[:, 2 * TOK],
        ],
        axis=0,
    )
    bands = lax.all_gather(
        plane.astype(jnp.float16), "seq", axis_index_groups=Y_GROUPS, tiled=True
    )
    ids = bands.reshape(NY, BAND, HD)[:, 2 * PLANE :].reshape(NY * NZ, HD).astype(jnp.float32)
    bands = bands.astype(jnp.bfloat16)

    attended = pl.pallas_call(
        attend,
        out_shape=jax.ShapeDtypeStruct((TOK, GROUP * HD), jnp.bfloat16),
        in_specs=[VMEM] * 3,
        out_specs=VMEM,
        scratch_shapes=[pltpu.VMEM((CHUNKS, GROUP * TOK, CHUNK), jnp.float32)],
        compiler_params=pltpu.CompilerParams(vmem_limit_bytes=24 * 1024 * 1024),
        cost_estimate=pl.CostEstimate(
            flops=4 * GROUP * TOK * CHUNKS * CHUNK * HD,
            bytes_accessed=3 * 1024 * 1024,
            transcendentals=GROUP * TOK * CHUNKS * CHUNK,
        ),
    )(queries, bands, ids)

    rows = lax.all_gather(
        attended.astype(jnp.float16), "seq", axis_index_groups=Z_GROUPS, tiled=True
    ).astype(jnp.bfloat16)

    def projected(own, *operands):
        return pl.pallas_call(
            functools.partial(project, own),
            out_shape=jax.ShapeDtypeStruct((NY * NX, TOK, 2 * width), jnp.bfloat16),
            in_specs=[VMEM] * (1 + len(operands)),
            out_specs=VMEM,
            scratch_shapes=[pltpu.VMEM((PLANE // 2, GROUP * HD), jnp.bfloat16)],
            compiler_params=pltpu.CompilerParams(vmem_limit_bytes=24 * 1024 * 1024),
            cost_estimate=pl.CostEstimate(
                flops=PLANE * GROUP * HD * NY * width,
                bytes_accessed=6 * 1024 * 1024,
                transcendentals=0,
            ),
        )(rows, *operands)

    theirs = lax.ppermute(projected(False, weights), "tp", CORE_SWAP)
    sums = projected(True, weights, theirs)
    parts = lax.all_to_all(
        sums, ("seq", "tp"), 0, 0, axis_index_groups=PLANE_GROUPS, tiled=True
    )
    return pl.pallas_call(
        combine,
        out_shape=jax.ShapeDtypeStruct((8 * TOK, width), jnp.bfloat16),
        in_specs=[VMEM],
        out_specs=VMEM,
        compiler_params=pltpu.CompilerParams(vmem_limit_bytes=16 * 1024 * 1024),
    )(parts)


def solution(mesh):
    return jax.shard_map(
        body,
        mesh=mesh,
        in_specs=(P("seq", "tp"), P("seq", "tp"), P("seq", "tp"), P("seq"), P("tp", "seq")),
        out_specs=P("tp", "seq"),
        check_vma=False,
    )
```

```python
import functools
import math

import jax
import jax.numpy as jnp
from jax import lax
from jax.experimental import pallas as pl
from jax.experimental.pallas import tpu as pltpu
from jax.sharding import PartitionSpec as P

HD = 128
GROUP = 8
TOK = 64
NY, NZ, NX, NC = 4, 16, 4, 2
CHUNK = 4 * TOK
CHUNKS = 9
PLANE = NZ * TOK
SEG_ROWS = 16
BAND = 2 * PLANE + SEG_ROWS
MASKED = -1e30
VMEM = pl.BlockSpec(memory_space=pltpu.VMEM)

Y_GROUPS = [[y * NZ + z for y in range(NY)] for z in range(NZ)]
Z_GROUPS = [[y * NZ + z for z in range(NZ)] for y in range(NY)]
CORE_SWAP = [(t, t ^ 1) for t in range(NX * NC)]


def flat(y, z, x, c):
    return ((y * NZ + z) * NX + x) * NC + c


PLANE_GROUPS = [
    [flat(y, z, x, c) for y in range(NY) for x in range(NX)] for z in range(NZ) for c in range(NC)
]
QUERY_MOVE = [(y * NZ + z, (y - z) % NY * NZ + z) for y in range(NY) for z in range(NZ)]


def y_flip(d):
    return [(y * NZ + z, (y ^ d) * NZ + z) for y in range(NY) for z in range(NZ)]


def attend(q_ref, kv_ref, ids_ref, out_ref, score_ref):
    at_y, at_z = lax.axis_index("seq") // NZ, lax.axis_index("seq") % NZ
    rank = (at_y + at_z) % NY * NZ + at_z
    first_pair = jnp.maximum(rank // 2 - (2 * CHUNKS - 1), 0)
    pairs = ids_ref[...]
    ids = pairs[:, :TOK] + 128.0 * pairs[:, TOK:]
    own = ids_ref[pl.ds(rank, 1), :]
    own = own[:, :TOK] + 128.0 * own[:, TOK:]
    rows = lax.broadcasted_iota(jnp.int32, (TOK, TOK), 0)
    cols = lax.broadcasted_iota(jnp.int32, (TOK, TOK), 1)
    across = jnp.broadcast_to(own, (TOK, TOK))
    down = jnp.sum(jnp.where(rows == cols, across, 0.0), axis=1, keepdims=True)
    below = jnp.sum((across < down).astype(jnp.float32), axis=1, keepdims=True)
    head_id = jnp.min(own, axis=1, keepdims=True)
    earlier = jnp.sum(((ids == head_id) & (rows < rank)).astype(jnp.float32))
    begin = (rank * TOK).astype(jnp.float32) + jnp.where(down == head_id, -earlier, below)
    begin = begin.astype(jnp.int32)
    position = rank * TOK + lax.broadcasted_iota(jnp.int32, (TOK, 1), 0)

    queries = jnp.concatenate([q_ref[:, g * HD : (g + 1) * HD] for g in range(GROUP)], axis=0)
    best = jnp.full((GROUP * TOK, HD), MASKED, jnp.float32)

    def rows_at(i, offset):
        parts = []
        for pair in (first_pair + 2 * i, first_pair + 2 * i + 1):
            start = pair // 8 * BAND + pair % 8 * (2 * TOK) + offset
            parts.append(kv_ref[pl.ds(pl.multiple_of(start, 16), 2 * TOK), :])
        return jnp.concatenate(parts, axis=0)

    for i in range(CHUNKS):
        scores = lax.dot_general(
            queries,
            rows_at(i, 0),
            (((1,), (1,)), ((), ())),
            preferred_element_type=jnp.float32,
        )
        at = first_pair * (2 * TOK) + i * CHUNK + lax.broadcasted_iota(jnp.int32, (TOK, CHUNK), 1)
        keep = (at >= begin) & (at <= position)
        scores = jnp.where(keep[None], scores.reshape(GROUP, TOK, CHUNK), MASKED)
        scores = scores.reshape(GROUP * TOK, CHUNK)
        score_ref[i] = scores
        best = jnp.maximum(best, jnp.maximum(scores[:, :HD], scores[:, HD:]))
    scale = math.log2(math.e) / math.sqrt(HD)
    top = jnp.max(best, axis=1, keepdims=True) * scale
    total = jnp.zeros((GROUP * TOK, HD), jnp.float32)
    mixed = jnp.zeros((GROUP * TOK, HD), jnp.float32)
    for i in range(CHUNKS):
        weights = jnp.exp2(score_ref[i] * scale - top)
        total += weights[:, :HD] + weights[:, HD:]
        mixed += jnp.dot(
            weights.astype(jnp.bfloat16),
            rows_at(i, PLANE),
            preferred_element_type=jnp.float32,
        )
    result = (mixed / jnp.sum(total, axis=1, keepdims=True)).astype(jnp.bfloat16)
    for g in range(GROUP):
        out_ref[:, g * HD : (g + 1) * HD] = result[g * TOK : (g + 1) * TOK]


def project(own, rows_ref, weight_ref, *refs):
    out_ref, picked_ref = refs[-2:]
    at_y, core = lax.axis_index("seq") // NZ, lax.axis_index("tp") % NC
    half = core if own else 1 - core
    for x in range(NX):
        for j in range(2):
            block = (2 * half + j) * 4 + (x + NY - at_y) % NY
            source = pl.ds(pl.multiple_of(block * TOK, TOK), TOK)
            picked_ref[pl.ds((2 * x + j) * TOK, TOK), :] = rows_ref[source, :]
    for d in range(NY):
        part = jnp.dot(picked_ref[...], weight_ref[d], preferred_element_type=jnp.float32)
        width = part.shape[-1]
        part = part.reshape(NX, 2, TOK, width)
        spot = pl.ds(d * NX, NX)
        for j in range(2):
            across = slice(j * width, (j + 1) * width)
            half_part = part[:, j]
            if own:
                half_part += refs[0][spot, :, across].astype(jnp.float32)
            out_ref[spot, :, across] = half_part.astype(jnp.bfloat16)


def combine(parts_ref, out_ref):
    at_x = lax.axis_index("tp") // NC
    width = out_ref.shape[1]
    for y in range(NY):
        total = parts_ref[y * NX].astype(jnp.float32)
        for x in range(1, NX):
            total += parts_ref[y * NX + x].astype(jnp.float32)
        total = total.astype(jnp.bfloat16)
        for j in range(2):
            block = 4 * j + (at_x + NY - y) % NY
            spot = pl.ds(pl.multiple_of(block * TOK, TOK), TOK)
            out_ref[spot, :] = total[:, j * width : (j + 1) * width]


def body(queries, keys, values, segment_ids, out_weight):
    width = out_weight.shape[1]
    copies = jnp.broadcast_to(out_weight[None], (NY,) + out_weight.shape)
    weights = lax.all_to_all(copies, "seq", 0, 0, axis_index_groups=Y_GROUPS, tiled=True)
    queries = lax.ppermute(queries, "seq", QUERY_MOVE)

    tag = jnp.concatenate([segment_ids % 128, segment_ids // 128])[None]
    tag = jnp.pad(tag, ((0, SEG_ROWS - 1), (0, 0))).astype(jnp.bfloat16)
    message = jnp.concatenate([keys, values, tag], axis=0)
    plane = lax.all_gather(message, "seq", axis_index_groups=Z_GROUPS)
    plane = jnp.concatenate(
        [
            plane[:, :TOK].reshape(PLANE, HD),
            plane[:, TOK : 2 * TOK].reshape(PLANE, HD),
            plane[:, 2 * TOK],
        ],
        axis=0,
    )
    bands = lax.all_gather(
        plane.astype(jnp.float16), "seq", axis_index_groups=Y_GROUPS, tiled=True
    )
    ids = bands.reshape(NY, BAND, HD)[:, 2 * PLANE :].reshape(NY * NZ, HD).astype(jnp.float32)
    bands = bands.astype(jnp.bfloat16)

    attended = pl.pallas_call(
        attend,
        out_shape=jax.ShapeDtypeStruct((TOK, GROUP * HD), jnp.bfloat16),
        in_specs=[VMEM] * 3,
        out_specs=VMEM,
        scratch_shapes=[pltpu.VMEM((CHUNKS, GROUP * TOK, CHUNK), jnp.float32)],
        compiler_params=pltpu.CompilerParams(vmem_limit_bytes=16 * 1024 * 1024),
        cost_estimate=pl.CostEstimate(
            flops=4 * GROUP * TOK * CHUNKS * CHUNK * HD,
            bytes_accessed=3 * 1024 * 1024,
            transcendentals=GROUP * TOK * CHUNKS * CHUNK,
        ),
    )(queries, bands, ids)

    attended, weights = lax.optimization_barrier((attended, weights))
    rows = lax.all_gather(
        attended.astype(jnp.float16), "seq", axis_index_groups=Z_GROUPS, tiled=True
    ).astype(jnp.bfloat16)

    def projected(own, *operands):
        return pl.pallas_call(
            functools.partial(project, own),
            out_shape=jax.ShapeDtypeStruct((NY * NX, TOK, 2 * width), jnp.bfloat16),
            in_specs=[VMEM] * (1 + len(operands)),
            out_specs=VMEM,
            scratch_shapes=[pltpu.VMEM((PLANE // 2, GROUP * HD), jnp.bfloat16)],
            compiler_params=pltpu.CompilerParams(vmem_limit_bytes=16 * 1024 * 1024),
            cost_estimate=pl.CostEstimate(
                flops=PLANE * GROUP * HD * NY * width,
                bytes_accessed=6 * 1024 * 1024,
                transcendentals=0,
            ),
        )(rows, *operands)

    theirs = lax.ppermute(projected(False, weights), "tp", CORE_SWAP)
    sums = projected(True, weights, theirs)
    parts = lax.all_to_all(
        sums, ("seq", "tp"), 0, 0, axis_index_groups=PLANE_GROUPS, tiled=True
    )
    return pl.pallas_call(
        combine,
        out_shape=jax.ShapeDtypeStruct((8 * TOK, width), jnp.bfloat16),
        in_specs=[VMEM],
        out_specs=VMEM,
        compiler_params=pltpu.CompilerParams(vmem_limit_bytes=16 * 1024 * 1024),
    )(parts)


def solution(mesh):
    return jax.shard_map(
        body,
        mesh=mesh,
        in_specs=(P("seq", "tp"), P("seq", "tp"), P("seq", "tp"), P("seq"), P("tp", "seq")),
        out_specs=P("tp", "seq"),
        check_vma=False,
    )
```

```python
import functools
import math

import jax
import jax.numpy as jnp
from jax import lax
from jax.experimental import pallas as pl
from jax.experimental.pallas import tpu as pltpu
from jax.sharding import PartitionSpec as P

HD = 128
GROUP = 8
TOK = 64
NY, NZ, NX, NC = 4, 16, 4, 2
CHUNK = 4 * TOK
CHUNKS = NZ // 4
HEADS_AT_ONCE = 4
PLANE = NZ * TOK
SEG_ROWS = 16
WEIGHT_ROWS = GROUP * HD
QUERY_ROWS = GROUP * TOK // 2
SENT_ROWS = WEIGHT_ROWS + QUERY_ROWS + SEG_ROWS
WIDE = GROUP * HD + 128
MASKED = -1e30
VMEM = pl.BlockSpec(memory_space=pltpu.VMEM)
ANY = pl.BlockSpec(memory_space=pl.ANY)

Y_GROUPS = [[y * NZ + z for y in range(NY)] for z in range(NZ)]
Z_GROUPS = [[y * NZ + z for z in range(NZ)] for y in range(NY)]
CORE_SWAP = [(t, t ^ 1) for t in range(NX * NC)]


def flat(y, z, x, c):
    return ((y * NZ + z) * NX + x) * NC + c


PLANE_GROUPS = [
    [flat(y, z, x, c) for y in range(NY) for x in range(NX)] for z in range(NZ) for c in range(NC)
]
def attend(sent_ref, plane_ref, out_ref, score_ref):
    at_y, at_z = lax.axis_index("seq") // NZ, lax.axis_index("seq") % NZ
    scale = math.log2(math.e) / math.sqrt(HD)
    count = HEADS_AT_ONCE * TOK
    rows = lax.broadcasted_iota(jnp.int32, (TOK, TOK), 0)
    cols = lax.broadcasted_iota(jnp.int32, (TOK, TOK), 1)
    lane = lax.broadcasted_iota(jnp.int32, (TOK, 128), 1)
    position = at_z * TOK + lax.broadcasted_iota(jnp.int32, (TOK, 1), 0)

    def ids_of(tile):
        pair = tile.astype(jnp.float32)[:1, : 2 * TOK]
        return pair[:, :TOK] + 128.0 * pair[:, TOK:]

    def part_of(i, start):
        return jnp.concatenate(
            [plane_ref[4 * i + j, start : start + TOK] for j in range(4)], axis=0
        )

    def key_ids(i):
        return jnp.concatenate(
            [ids_of(plane_ref[4 * i + j, 2 * TOK :]) for j in range(4)], axis=1
        )

    def band(ahead, chunks):
        y = at_y + ahead
        slot = (y + NY - at_z % NY) % NY
        own = ids_of(sent_ref[y, WEIGHT_ROWS + QUERY_ROWS :, :])
        own = jnp.sum(jnp.where(rows == cols, own, 0.0), axis=1, keepdims=True)
        keys = [part_of(i, 0) for i in chunks]
        values = [part_of(i, TOK) for i in chunks]
        keeps = []
        for i in chunks:
            keep = key_ids(i) == own
            if ahead == 0:
                at = i * CHUNK + lax.broadcasted_iota(jnp.int32, (TOK, CHUNK), 1)
                keep = keep & (at <= position)
            keeps.append(keep)
        marks = jnp.zeros((TOK, 128), jnp.float32)
        for first in range(0, GROUP, HEADS_AT_ONCE):
            heads = range(first, first + HEADS_AT_ONCE)
            queries = []
            for g in heads:
                row = WEIGHT_ROWS + g // 2 * TOK
                queries.append(sent_ref[y, row : row + TOK, g % 2 * HD : (g % 2 + 1) * HD])
            queries = jnp.concatenate(queries, axis=0)
            held = slice(first * TOK, first * TOK + count)
            best = jnp.full((count, HD), MASKED, jnp.float32)
            for n in range(len(chunks)):
                scores = lax.dot_general(
                    queries, keys[n], (((1,), (1,)), ((), ())), preferred_element_type=jnp.float32
                )
                scores = scores.reshape(HEADS_AT_ONCE, TOK, CHUNK)
                scores = jnp.where(keeps[n][None], scores, MASKED).reshape(count, CHUNK)
                score_ref[n, held] = scores
                best = jnp.maximum(best, jnp.maximum(scores[:, :HD], scores[:, HD:]))
            top = jnp.max(best, axis=1, keepdims=True) * scale
            total = jnp.zeros((count, HD), jnp.float32)
            mixed = jnp.zeros((count, HD), jnp.float32)
            for n in range(len(chunks)):
                weights = jnp.exp2(score_ref[n, held] * scale - top)
                total += weights[:, :HD] + weights[:, HD:]
                mixed += jnp.dot(
                    weights.astype(jnp.bfloat16), values[n], preferred_element_type=jnp.float32
                )
            total = jnp.sum(total, axis=1, keepdims=True)
            result = (mixed / total).astype(jnp.bfloat16)
            level = top + jnp.log2(total)
            high = level.astype(jnp.bfloat16).astype(jnp.float32)
            middle = (level - high).astype(jnp.bfloat16).astype(jnp.float32)
            for place, g in enumerate(heads):
                here = slice(place * TOK, (place + 1) * TOK)
                out_ref[slot, :, g * HD : (g + 1) * HD] = result[here]
                marks = jnp.where(lane == g, high[here], marks)
                marks = jnp.where(lane == GROUP + g, middle[here], marks)
                rest = level[here] - high[here] - middle[here]
                marks = jnp.where(lane == 2 * GROUP + g, rest, marks)
        out_ref[slot, :, GROUP * HD :] = marks.astype(jnp.bfloat16)

    for ahead in range(NY):
        seen = at_y + ahead < NY
        if ahead == 3:
            seen = seen & (at_z == 0)

        @pl.when(seen)
        def _(ahead=ahead):
            band(ahead, list(range(CHUNKS)) if ahead < 3 else [CHUNKS - 1])

        @pl.when(jnp.logical_not(seen))
        def _(ahead=ahead):
            slot = (at_y + ahead + NY - at_z % NY) % NY
            out_ref[slot, :, : GROUP * HD] = jnp.zeros((TOK, GROUP * HD), jnp.bfloat16)
            marks = jnp.where(lane < GROUP, MASKED, 0.0)
            out_ref[slot, :, GROUP * HD :] = marks.astype(jnp.bfloat16)


def merge(parts_ref, out_ref):
    levels = []
    for y in range(NY):
        marks = parts_ref[y, :, GROUP * HD :].astype(jnp.float32)
        levels.append(
            marks[:, :GROUP] + marks[:, GROUP : 2 * GROUP] + marks[:, 2 * GROUP : 3 * GROUP]
        )
    top = functools.reduce(jnp.maximum, levels)
    shares = [jnp.exp2(level - top) for level in levels]
    whole = sum(shares)
    shares = [share / whole for share in shares]
    for g in range(GROUP):
        across = slice(g * HD, (g + 1) * HD)
        total = jnp.zeros((TOK, HD), jnp.float32)
        for y in range(NY):
            total += shares[y][:, g : g + 1] * parts_ref[y, :, across].astype(jnp.float32)
        out_ref[:, across] = total.astype(jnp.bfloat16)


def project(own, rows_ref, weight_ref, *refs):
    out_ref, picked_ref = refs[-2:]
    at_y, core = lax.axis_index("seq") // NZ, lax.axis_index("tp") % NC
    half = core if own else 1 - core
    for x in range(NX):
        for j in range(2):
            block = (2 * half + j) * 4 + (x + NY - at_y) % NY
            source = pl.ds(pl.multiple_of(block * TOK, TOK), TOK)
            picked_ref[pl.ds((2 * x + j) * TOK, TOK), :] = rows_ref[source, :]
    for d in range(NY):
        part = jnp.dot(picked_ref[...], weight_ref[d, :WEIGHT_ROWS], preferred_element_type=jnp.float32)
        width = part.shape[-1]
        part = part.reshape(NX, 2, TOK, width)
        spot = pl.ds(d * NX, NX)
        for j in range(2):
            across = slice(j * width, (j + 1) * width)
            half_part = part[:, j]
            if own:
                half_part += refs[0][spot, :, across].astype(jnp.float32)
            out_ref[spot, :, across] = half_part.astype(jnp.bfloat16)


def combine(parts_ref, out_ref):
    at_x = lax.axis_index("tp") // NC
    width = out_ref.shape[1]
    for y in range(NY):
        total = parts_ref[y * NX].astype(jnp.float32)
        for x in range(1, NX):
            total += parts_ref[y * NX + x].astype(jnp.float32)
        total = total.astype(jnp.bfloat16)
        for j in range(2):
            block = 4 * j + (at_x + NY - y) % NY
            spot = pl.ds(pl.multiple_of(block * TOK, TOK), TOK)
            out_ref[spot, :] = total[:, j * width : (j + 1) * width]


def spread(weight_ref, q_ref, ids_ref, out_ref, held_ref, own_ref, in_sems, out_sems):
    width = weight_ref.shape[1]
    half = WEIGHT_ROWS // 2
    arrivals = []
    for piece in range(2):
        part = pl.ds(piece * half, half)
        copy = pltpu.make_async_copy(weight_ref.at[part], held_ref.at[part], in_sems.at[piece])
        arrivals.append((part, [copy]))
    pieces = []
    for k in range(q_ref.shape[1] // width):
        target = held_ref.at[pl.ds(WEIGHT_ROWS + k * TOK, TOK)]
        source = q_ref.at[:, pl.ds(k * width, width)]
        pieces.append(pltpu.make_async_copy(source, target, in_sems.at[2 + k]))
    arrivals.append((pl.ds(WEIGHT_ROWS, SENT_ROWS - WEIGHT_ROWS), pieces))
    fetch = pltpu.make_async_copy(ids_ref, own_ref, in_sems.at[6])
    fetch.start()
    for _, copies in arrivals:
        for copy in copies:
            copy.start()
    leaving = []
    for index, (part, copies) in enumerate(arrivals):
        for copy in copies:
            copy.wait()
        if index == 2:
            fetch.wait()
            ids = own_ref[...]
            both = jnp.concatenate([ids & 127, ids >> 7, ids & 0, ids & 0], axis=1)
            both = jnp.broadcast_to(both.astype(jnp.float32), (SEG_ROWS, width))
            held_ref[WEIGHT_ROWS + QUERY_ROWS :] = both.astype(jnp.bfloat16)
        for y in range(NY):
            copy = pltpu.make_async_copy(
                held_ref.at[part], out_ref.at[y, part], out_sems.at[index, y]
            )
            copy.start()
            leaving.append(copy)
    for copy in leaving:
        copy.wait()


def body(queries, keys, values, segment_ids, out_weight):
    width = out_weight.shape[1]
    copies = pl.pallas_call(
        spread,
        out_shape=jax.ShapeDtypeStruct((NY, SENT_ROWS, width), jnp.bfloat16),
        in_specs=[ANY] * 3,
        out_specs=ANY,
        scratch_shapes=[
            pltpu.VMEM((SENT_ROWS, width), jnp.bfloat16),
            pltpu.VMEM((1, TOK), jnp.int32),
            pltpu.SemaphoreType.DMA((7,)),
            pltpu.SemaphoreType.DMA((3, NY)),
        ],
        compiler_params=pltpu.CompilerParams(vmem_limit_bytes=60 * 1024 * 1024),
    )(out_weight, queries, segment_ids.reshape(1, TOK))
    sent = lax.all_to_all(copies, "seq", 0, 0, axis_index_groups=Y_GROUPS, tiled=True)

    tag = jnp.concatenate([segment_ids % 128, segment_ids // 128])[None]
    tag = jnp.pad(tag, ((0, SEG_ROWS - 1), (0, 0))).astype(jnp.bfloat16)
    message = jnp.concatenate([keys, values, tag], axis=0)
    plane = lax.all_gather(message, "seq", axis_index_groups=Z_GROUPS)

    parts = pl.pallas_call(
        attend,
        out_shape=jax.ShapeDtypeStruct((NY, TOK, WIDE), jnp.bfloat16),
        in_specs=[VMEM] * 2,
        out_specs=VMEM,
        scratch_shapes=[pltpu.VMEM((CHUNKS, GROUP * TOK, CHUNK), jnp.float32)],
        compiler_params=pltpu.CompilerParams(vmem_limit_bytes=16 * 1024 * 1024),
        cost_estimate=pl.CostEstimate(
            flops=12 * GROUP * TOK * CHUNKS * CHUNK * HD,
            bytes_accessed=3 * 1024 * 1024,
            transcendentals=3 * GROUP * TOK * CHUNKS * CHUNK,
        ),
    )(sent, plane)
    parts = lax.all_to_all(parts, "seq", 0, 0, axis_index_groups=Y_GROUPS, tiled=True)
    attended = pl.pallas_call(
        merge,
        out_shape=jax.ShapeDtypeStruct((TOK, GROUP * HD), jnp.bfloat16),
        in_specs=[VMEM],
        out_specs=VMEM,
        compiler_params=pltpu.CompilerParams(vmem_limit_bytes=16 * 1024 * 1024),
    )(parts)

    rows = lax.all_gather(
        attended.astype(jnp.float16), "seq", axis_index_groups=Z_GROUPS, tiled=True
    ).astype(jnp.bfloat16)

    def projected(own, *operands):
        return pl.pallas_call(
            functools.partial(project, own),
            out_shape=jax.ShapeDtypeStruct((NY * NX, TOK, 2 * width), jnp.bfloat16),
            in_specs=[VMEM] * (1 + len(operands)),
            out_specs=VMEM,
            scratch_shapes=[pltpu.VMEM((PLANE // 2, GROUP * HD), jnp.bfloat16)],
            compiler_params=pltpu.CompilerParams(vmem_limit_bytes=16 * 1024 * 1024),
            cost_estimate=pl.CostEstimate(
                flops=PLANE * GROUP * HD * NY * width,
                bytes_accessed=6 * 1024 * 1024,
                transcendentals=0,
            ),
        )(rows, *operands)

    theirs = lax.ppermute(projected(False, sent), "tp", CORE_SWAP)
    sums = projected(True, sent, theirs)
    parts = lax.all_to_all(
        sums, ("seq", "tp"), 0, 0, axis_index_groups=PLANE_GROUPS, tiled=True
    )
    return pl.pallas_call(
        combine,
        out_shape=jax.ShapeDtypeStruct((8 * TOK, width), jnp.bfloat16),
        in_specs=[VMEM],
        out_specs=VMEM,
        compiler_params=pltpu.CompilerParams(vmem_limit_bytes=16 * 1024 * 1024),
    )(parts)


def solution(mesh):
    return jax.shard_map(
        body,
        mesh=mesh,
        in_specs=(P("seq", "tp"), P("seq", "tp"), P("seq", "tp"), P("seq"), P("tp", "seq")),
        out_specs=P("tp", "seq"),
        check_vma=False,
    )
```

```python
import functools
import math

import jax
import jax.numpy as jnp
from jax import lax
from jax.experimental import pallas as pl
from jax.experimental.pallas import tpu as pltpu
from jax.sharding import PartitionSpec as P

HD = 128
GROUP = 8
TOK = 64
NY, NZ, NX, NC = 4, 16, 4, 2
CHUNK = 4 * TOK
CHUNKS = NZ // 4
HEADS_AT_ONCE = 4
PLANE = NZ * TOK
SEG_ROWS = 16
WEIGHT_ROWS = GROUP * HD
QUERY_ROWS = GROUP * TOK // 2
SENT_ROWS = WEIGHT_ROWS + QUERY_ROWS + SEG_ROWS
WIDE = GROUP * HD + 128
MASKED = -1e30
VMEM = pl.BlockSpec(memory_space=pltpu.VMEM)
ANY = pl.BlockSpec(memory_space=pl.ANY)

Y_GROUPS = [[y * NZ + z for y in range(NY)] for z in range(NZ)]
Z_GROUPS = [[y * NZ + z for z in range(NZ)] for y in range(NY)]
CORE_SWAP = [(t, t ^ 1) for t in range(NX * NC)]


def flat(y, z, x, c):
    return ((y * NZ + z) * NX + x) * NC + c


PLANE_GROUPS = [
    [flat(y, z, x, c) for y in range(NY) for x in range(NX)] for z in range(NZ) for c in range(NC)
]
def attend(sent_ref, plane_ref, out_ref, score_ref):
    at_y, at_z = lax.axis_index("seq") // NZ, lax.axis_index("seq") % NZ
    scale = math.log2(math.e) / math.sqrt(HD)
    count = HEADS_AT_ONCE * TOK
    rows = lax.broadcasted_iota(jnp.int32, (TOK, TOK), 0)
    cols = lax.broadcasted_iota(jnp.int32, (TOK, TOK), 1)
    lane = lax.broadcasted_iota(jnp.int32, (TOK, 128), 1)
    position = at_z * TOK + lax.broadcasted_iota(jnp.int32, (TOK, 1), 0)

    def ids_of(tile):
        pair = tile.astype(jnp.float32)[:1, : 2 * TOK]
        return pair[:, :TOK] + 128.0 * pair[:, TOK:]

    def part_of(i, start):
        return jnp.concatenate(
            [plane_ref[4 * i + j, start : start + TOK] for j in range(4)], axis=0
        )

    def key_ids(i):
        return jnp.concatenate(
            [ids_of(plane_ref[4 * i + j, 2 * TOK :]) for j in range(4)], axis=1
        )

    def band(ahead, chunks):
        y = at_y + ahead
        slot = (y + NY - at_z % NY) % NY
        own = ids_of(sent_ref[y, WEIGHT_ROWS + QUERY_ROWS :, :])
        own = jnp.sum(jnp.where(rows == cols, own, 0.0), axis=1, keepdims=True)
        keys = [part_of(i, 0) for i in chunks]
        values = [part_of(i, TOK) for i in chunks]
        keeps = []
        for i in chunks:
            keep = key_ids(i) == own
            if ahead == 0:
                at = i * CHUNK + lax.broadcasted_iota(jnp.int32, (TOK, CHUNK), 1)
                keep = keep & (at <= position)
            keeps.append(keep)
        marks = jnp.zeros((TOK, 128), jnp.float32)
        for first in range(0, GROUP, HEADS_AT_ONCE):
            heads = range(first, first + HEADS_AT_ONCE)
            queries = []
            for g in heads:
                row = WEIGHT_ROWS + g // 2 * TOK
                queries.append(sent_ref[y, row : row + TOK, g % 2 * HD : (g % 2 + 1) * HD])
            queries = jnp.concatenate(queries, axis=0)
            held = slice(first * TOK, first * TOK + count)
            best = jnp.full((count, HD), MASKED, jnp.float32)
            for n in range(len(chunks)):
                scores = lax.dot_general(
                    queries, keys[n], (((1,), (1,)), ((), ())), preferred_element_type=jnp.float32
                )
                scores = scores.reshape(HEADS_AT_ONCE, TOK, CHUNK)
                scores = jnp.where(keeps[n][None], scores, MASKED).reshape(count, CHUNK)
                score_ref[n, held] = scores
                best = jnp.maximum(best, jnp.maximum(scores[:, :HD], scores[:, HD:]))
            top = jnp.max(best, axis=1, keepdims=True) * scale
            total = jnp.zeros((count, HD), jnp.float32)
            mixed = jnp.zeros((count, HD), jnp.float32)
            for n in range(len(chunks)):
                weights = jnp.exp2(score_ref[n, held] * scale - top)
                total += weights[:, :HD] + weights[:, HD:]
                mixed += jnp.dot(
                    weights.astype(jnp.bfloat16), values[n], preferred_element_type=jnp.float32
                )
            total = jnp.sum(total, axis=1, keepdims=True)
            result = (mixed / total).astype(jnp.bfloat16)
            level = top + jnp.log2(total)
            high = level.astype(jnp.bfloat16).astype(jnp.float32)
            middle = (level - high).astype(jnp.bfloat16).astype(jnp.float32)
            for place, g in enumerate(heads):
                here = slice(place * TOK, (place + 1) * TOK)
                out_ref[slot, :, g * HD : (g + 1) * HD] = result[here]
                marks = jnp.where(lane == g, high[here], marks)
                marks = jnp.where(lane == GROUP + g, middle[here], marks)
                rest = level[here] - high[here] - middle[here]
                marks = jnp.where(lane == 2 * GROUP + g, rest, marks)
        out_ref[slot, :, GROUP * HD :] = marks.astype(jnp.bfloat16)

    low = at_z < NZ // 2
    cases = [
        (0, low, [0, 1]),
        (0, jnp.logical_not(low), [0, 1, 2, 3]),
        (1, at_y >= 0, [0, 1, 2, 3]),
        (2, low, [0, 1, 2, 3]),
        (2, jnp.logical_not(low), [1, 2, 3]),
        (3, at_z == 0, [3]),
    ]
    for ahead, when, chunks in cases:

        @pl.when((at_y + ahead < NY) & when)
        def _(ahead=ahead, chunks=chunks):
            band(ahead, chunks)

    for ahead in range(1, NY):
        unseen = at_y + ahead >= NY
        if ahead == 3:
            unseen = unseen | (at_z != 0)

        @pl.when(unseen)
        def _(ahead=ahead):
            slot = (at_y + ahead + NY - at_z % NY) % NY
            out_ref[slot, :, : GROUP * HD] = jnp.zeros((TOK, GROUP * HD), jnp.bfloat16)
            marks = jnp.where(lane < GROUP, MASKED, 0.0)
            out_ref[slot, :, GROUP * HD :] = marks.astype(jnp.bfloat16)


def merge(parts_ref, out_ref):
    levels = []
    for y in range(NY):
        marks = parts_ref[y, :, GROUP * HD :].astype(jnp.float32)
        levels.append(
            marks[:, :GROUP] + marks[:, GROUP : 2 * GROUP] + marks[:, 2 * GROUP : 3 * GROUP]
        )
    top = functools.reduce(jnp.maximum, levels)
    shares = [jnp.exp2(level - top) for level in levels]
    whole = sum(shares)
    shares = [share / whole for share in shares]
    for g in range(GROUP):
        across = slice(g * HD, (g + 1) * HD)
        total = jnp.zeros((TOK, HD), jnp.float32)
        for y in range(NY):
            total += shares[y][:, g : g + 1] * parts_ref[y, :, across].astype(jnp.float32)
        out_ref[:, across] = total.astype(jnp.bfloat16)


def project(own, rows_ref, weight_ref, *refs):
    out_ref, picked_ref = refs[-2:]
    at_y, core = lax.axis_index("seq") // NZ, lax.axis_index("tp") % NC
    half = core if own else 1 - core
    for x in range(NX):
        for j in range(2):
            block = (2 * half + j) * 4 + (x + NY - at_y) % NY
            source = pl.ds(pl.multiple_of(block * TOK, TOK), TOK)
            picked_ref[pl.ds((2 * x + j) * TOK, TOK), :] = rows_ref[source, :]
    for d in range(NY):
        part = jnp.dot(picked_ref[...], weight_ref[d, :WEIGHT_ROWS], preferred_element_type=jnp.float32)
        width = part.shape[-1]
        part = part.reshape(NX, 2, TOK, width)
        spot = pl.ds(d * NX, NX)
        for j in range(2):
            across = slice(j * width, (j + 1) * width)
            half_part = part[:, j]
            out_ref[spot, :, across] = half_part.astype(out_ref.dtype)


def add(own_ref, added_ref, out_ref):
    for place in range(NY * NX):
        total = own_ref[place] + added_ref[place].astype(jnp.float32)
        out_ref[place] = total.astype(jnp.bfloat16)


def combine(parts_ref, out_ref):
    at_x = lax.axis_index("tp") // NC
    width = out_ref.shape[1]
    for y in range(NY):
        total = parts_ref[y * NX].astype(jnp.float32)
        for x in range(1, NX):
            total += parts_ref[y * NX + x].astype(jnp.float32)
        total = total.astype(jnp.bfloat16)
        for j in range(2):
            block = 4 * j + (at_x + NY - y) % NY
            spot = pl.ds(pl.multiple_of(block * TOK, TOK), TOK)
            out_ref[spot, :] = total[:, j * width : (j + 1) * width]


def spread(weight_ref, q_ref, ids_ref, out_ref, held_ref, own_ref, in_sems, out_sems):
    width = weight_ref.shape[1]
    half = WEIGHT_ROWS // 2
    arrivals = []
    for piece in range(2):
        part = pl.ds(piece * half, half)
        copy = pltpu.make_async_copy(weight_ref.at[part], held_ref.at[part], in_sems.at[piece])
        arrivals.append((part, [copy]))
    pieces = []
    for k in range(q_ref.shape[1] // width):
        target = held_ref.at[pl.ds(WEIGHT_ROWS + k * TOK, TOK)]
        source = q_ref.at[:, pl.ds(k * width, width)]
        pieces.append(pltpu.make_async_copy(source, target, in_sems.at[2 + k]))
    arrivals.append((pl.ds(WEIGHT_ROWS, SENT_ROWS - WEIGHT_ROWS), pieces))
    fetch = pltpu.make_async_copy(ids_ref, own_ref, in_sems.at[6])
    fetch.start()
    for _, copies in arrivals:
        for copy in copies:
            copy.start()
    leaving = []
    for index, (part, copies) in enumerate(arrivals):
        for copy in copies:
            copy.wait()
        if index == 2:
            fetch.wait()
            ids = own_ref[...]
            both = jnp.concatenate([ids & 127, ids >> 7, ids & 0, ids & 0], axis=1)
            both = jnp.broadcast_to(both.astype(jnp.float32), (SEG_ROWS, width))
            held_ref[WEIGHT_ROWS + QUERY_ROWS :] = both.astype(jnp.bfloat16)
        for y in range(NY):
            copy = pltpu.make_async_copy(
                held_ref.at[part], out_ref.at[y, part], out_sems.at[index, y]
            )
            copy.start()
            leaving.append(copy)
    for copy in leaving:
        copy.wait()


def body(queries, keys, values, segment_ids, out_weight):
    width = out_weight.shape[1]
    copies = pl.pallas_call(
        spread,
        out_shape=jax.ShapeDtypeStruct((NY, SENT_ROWS, width), jnp.bfloat16),
        in_specs=[ANY] * 3,
        out_specs=ANY,
        scratch_shapes=[
            pltpu.VMEM((SENT_ROWS, width), jnp.bfloat16),
            pltpu.VMEM((1, TOK), jnp.int32),
            pltpu.SemaphoreType.DMA((7,)),
            pltpu.SemaphoreType.DMA((3, NY)),
        ],
        compiler_params=pltpu.CompilerParams(vmem_limit_bytes=60 * 1024 * 1024),
    )(out_weight, queries, segment_ids.reshape(1, TOK))
    sent = lax.all_to_all(copies, "seq", 0, 0, axis_index_groups=Y_GROUPS, tiled=True)

    tag = jnp.concatenate([segment_ids % 128, segment_ids // 128])[None]
    tag = jnp.pad(tag, ((0, SEG_ROWS - 1), (0, 0))).astype(jnp.bfloat16)
    message = jnp.concatenate([keys, values, tag], axis=0)
    plane = lax.all_gather(message, "seq", axis_index_groups=Z_GROUPS)

    parts = pl.pallas_call(
        attend,
        out_shape=jax.ShapeDtypeStruct((NY, TOK, WIDE), jnp.bfloat16),
        in_specs=[VMEM] * 2,
        out_specs=VMEM,
        scratch_shapes=[pltpu.VMEM((CHUNKS, GROUP * TOK, CHUNK), jnp.float32)],
        compiler_params=pltpu.CompilerParams(vmem_limit_bytes=16 * 1024 * 1024),
        cost_estimate=pl.CostEstimate(
            flops=12 * GROUP * TOK * CHUNKS * CHUNK * HD,
            bytes_accessed=3 * 1024 * 1024,
            transcendentals=3 * GROUP * TOK * CHUNKS * CHUNK,
        ),
    )(sent, plane)
    parts = lax.all_to_all(parts, "seq", 0, 0, axis_index_groups=Y_GROUPS, tiled=True)
    attended = pl.pallas_call(
        merge,
        out_shape=jax.ShapeDtypeStruct((TOK, GROUP * HD), jnp.bfloat16),
        in_specs=[VMEM],
        out_specs=VMEM,
        compiler_params=pltpu.CompilerParams(vmem_limit_bytes=16 * 1024 * 1024),
    )(parts)

    rows = lax.all_gather(
        attended.astype(jnp.float16), "seq", axis_index_groups=Z_GROUPS, tiled=True
    ).astype(jnp.bfloat16)

    def projected(own, *operands):
        return pl.pallas_call(
            functools.partial(project, own),
            out_shape=jax.ShapeDtypeStruct(
                (NY * NX, TOK, 2 * width), jnp.float32 if own else jnp.bfloat16
            ),
            in_specs=[VMEM] * (1 + len(operands)),
            out_specs=VMEM,
            scratch_shapes=[pltpu.VMEM((PLANE // 2, GROUP * HD), jnp.bfloat16)],
            compiler_params=pltpu.CompilerParams(vmem_limit_bytes=16 * 1024 * 1024),
            cost_estimate=pl.CostEstimate(
                flops=PLANE * GROUP * HD * NY * width,
                bytes_accessed=6 * 1024 * 1024,
                transcendentals=0,
            ),
        )(rows, *operands)

    theirs = lax.ppermute(projected(False, sent), "tp", CORE_SWAP)
    sums = pl.pallas_call(
        add,
        out_shape=jax.ShapeDtypeStruct((NY * NX, TOK, 2 * width), jnp.bfloat16),
        in_specs=[VMEM] * 2,
        out_specs=VMEM,
        compiler_params=pltpu.CompilerParams(vmem_limit_bytes=16 * 1024 * 1024),
    )(projected(True, sent), theirs)
    parts = lax.all_to_all(
        sums, ("seq", "tp"), 0, 0, axis_index_groups=PLANE_GROUPS, tiled=True
    )
    return pl.pallas_call(
        combine,
        out_shape=jax.ShapeDtypeStruct((8 * TOK, width), jnp.bfloat16),
        in_specs=[VMEM],
        out_specs=VMEM,
        compiler_params=pltpu.CompilerParams(vmem_limit_bytes=16 * 1024 * 1024),
    )(parts)


def solution(mesh):
    return jax.shard_map(
        body,
        mesh=mesh,
        in_specs=(P("seq", "tp"), P("seq", "tp"), P("seq", "tp"), P("seq"), P("tp", "seq")),
        out_specs=P("tp", "seq"),
        check_vma=False,
    )
```

```python
import functools
import math

import jax
import jax.numpy as jnp
from jax import lax
from jax.experimental import pallas as pl
from jax.experimental.pallas import tpu as pltpu
from jax.sharding import PartitionSpec as P

HD = 128
GROUP = 8
TOK = 64
NY, NZ, NX, NC = 4, 16, 4, 2
CHUNK = 4 * TOK
CHUNKS = NZ // 4
HEADS_AT_ONCE = 4
PLANE = NZ * TOK
SEG_ROWS = 16
PIECES = 4
WEIGHT_ROWS = GROUP * HD
QUERY_ROWS = GROUP * TOK // 2
SENT_ROWS = WEIGHT_ROWS + QUERY_ROWS + SEG_ROWS
WIDE = GROUP * HD + 128
MASKED = -1e30
VMEM = pl.BlockSpec(memory_space=pltpu.VMEM)
ANY = pl.BlockSpec(memory_space=pl.ANY)

Y_GROUPS = [[y * NZ + z for y in range(NY)] for z in range(NZ)]
Z_GROUPS = [[y * NZ + z for z in range(NZ)] for y in range(NY)]
CORE_SWAP = [(t, t ^ 1) for t in range(NX * NC)]


def flat(y, z, x, c):
    return ((y * NZ + z) * NX + x) * NC + c


PLANE_GROUPS = [
    [flat(y, z, x, c) for x in range(NX) for y in range(NY)] for z in range(NZ) for c in range(NC)
]
def attend(sent_ref, plane_ref, out_ref, score_ref):
    at_y, at_z = lax.axis_index("seq") // NZ, lax.axis_index("seq") % NZ
    scale = math.log2(math.e) / math.sqrt(HD)
    count = HEADS_AT_ONCE * TOK
    rows = lax.broadcasted_iota(jnp.int32, (TOK, TOK), 0)
    cols = lax.broadcasted_iota(jnp.int32, (TOK, TOK), 1)
    lane = lax.broadcasted_iota(jnp.int32, (TOK, 128), 1)
    position = at_z * TOK + lax.broadcasted_iota(jnp.int32, (TOK, 1), 0)

    def ids_of(tile):
        pair = tile.astype(jnp.float32)[:1, : 2 * TOK]
        return pair[:, :TOK] + 128.0 * pair[:, TOK:]

    def part_of(i, start):
        return jnp.concatenate(
            [plane_ref[4 * i + j, start : start + TOK] for j in range(4)], axis=0
        )

    def key_ids(i):
        return jnp.concatenate(
            [ids_of(plane_ref[4 * i + j, 2 * TOK :]) for j in range(4)], axis=1
        )

    all_key_ids = [key_ids(i) for i in range(CHUNKS)]

    def band(ahead, chunks):
        y = at_y + ahead
        slot = (y + NY - at_z % NY) % NY
        own = ids_of(sent_ref[y, WEIGHT_ROWS + QUERY_ROWS :, :])
        own = jnp.sum(jnp.where(rows == cols, own, 0.0), axis=1, keepdims=True)
        keys = [part_of(i, 0) for i in chunks]
        values = [part_of(i, TOK) for i in chunks]
        keeps = []
        for i in chunks:
            keep = all_key_ids[i] == own
            if ahead == 0:
                at = i * CHUNK + lax.broadcasted_iota(jnp.int32, (TOK, CHUNK), 1)
                keep = keep & (at <= position)
            keeps.append(keep)
        marks = jnp.zeros((TOK, 128), jnp.float32)
        for first in range(0, GROUP, HEADS_AT_ONCE):
            heads = range(first, first + HEADS_AT_ONCE)
            queries = []
            for g in heads:
                row = WEIGHT_ROWS + g // 2 * TOK
                queries.append(sent_ref[y, row : row + TOK, g % 2 * HD : (g % 2 + 1) * HD])
            queries = jnp.concatenate(queries, axis=0)
            held = slice(first * TOK, first * TOK + count)
            best = jnp.full((count, HD), MASKED, jnp.float32)
            for n in range(len(chunks)):
                scores = lax.dot_general(
                    queries, keys[n], (((1,), (1,)), ((), ())), preferred_element_type=jnp.float32
                )
                scores = scores.reshape(HEADS_AT_ONCE, TOK, CHUNK)
                scores = jnp.where(keeps[n][None], scores, MASKED).reshape(count, CHUNK)
                score_ref[n, held] = scores
                best = jnp.maximum(best, jnp.maximum(scores[:, :HD], scores[:, HD:]))
            top = jnp.max(best, axis=1, keepdims=True) * scale
            total = jnp.zeros((count, HD), jnp.float32)
            mixed = jnp.zeros((count, HD), jnp.float32)
            for n in range(len(chunks)):
                weights = jnp.exp2(score_ref[n, held] * scale - top)
                total += weights[:, :HD] + weights[:, HD:]
                mixed += jnp.dot(
                    weights.astype(jnp.bfloat16), values[n], preferred_element_type=jnp.float32
                )
            total = jnp.sum(total, axis=1, keepdims=True)
            result = (mixed / total).astype(jnp.bfloat16)
            level = top + jnp.log2(total)
            high = level.astype(jnp.bfloat16).astype(jnp.float32)
            middle = (level - high).astype(jnp.bfloat16).astype(jnp.float32)
            for place, g in enumerate(heads):
                here = slice(place * TOK, (place + 1) * TOK)
                out_ref[slot, :, g * HD : (g + 1) * HD] = result[here]
                marks = jnp.where(lane == g, high[here], marks)
                marks = jnp.where(lane == GROUP + g, middle[here], marks)
                rest = level[here] - high[here] - middle[here]
                marks = jnp.where(lane == 2 * GROUP + g, rest, marks)
        out_ref[slot, :, GROUP * HD :] = marks.astype(jnp.bfloat16)

    low = at_z < NZ // 2
    cases = [
        (0, low, [0, 1]),
        (0, jnp.logical_not(low), [0, 1, 2, 3]),
        (1, at_y >= 0, [0, 1, 2, 3]),
        (2, low, [0, 1, 2, 3]),
        (2, jnp.logical_not(low), [1, 2, 3]),
        (3, at_z == 0, [3]),
    ]
    for ahead, when, chunks in cases:

        @pl.when((at_y + ahead < NY) & when)
        def _(ahead=ahead, chunks=chunks):
            band(ahead, chunks)

    for ahead in range(1, NY):
        unseen = at_y + ahead >= NY
        if ahead == 3:
            unseen = unseen | (at_z != 0)

        @pl.when(unseen)
        def _(ahead=ahead):
            slot = (at_y + ahead + NY - at_z % NY) % NY
            out_ref[slot, :, : GROUP * HD] = jnp.zeros((TOK, GROUP * HD), jnp.bfloat16)
            marks = jnp.where(lane < GROUP, MASKED, 0.0)
            out_ref[slot, :, GROUP * HD :] = marks.astype(jnp.bfloat16)


def merge(parts_ref, out_ref):
    levels = []
    for y in range(NY):
        marks = parts_ref[y, :, GROUP * HD :].astype(jnp.float32)
        levels.append(
            marks[:, :GROUP] + marks[:, GROUP : 2 * GROUP] + marks[:, 2 * GROUP : 3 * GROUP]
        )
    top = functools.reduce(jnp.maximum, levels)
    shares = [jnp.exp2(level - top) for level in levels]
    whole = sum(shares)
    shares = [share / whole for share in shares]
    for g in range(GROUP):
        across = slice(g * HD, (g + 1) * HD)
        total = jnp.zeros((TOK, HD), jnp.float32)
        for y in range(NY):
            total += shares[y][:, g : g + 1] * parts_ref[y, :, across].astype(jnp.float32)
        out_ref[:, across] = total.astype(jnp.bfloat16)


def project(own, rows_ref, weight_ref, *refs):
    out_ref, picked_ref = refs[-2:]
    at_y, core = lax.axis_index("seq") // NZ, lax.axis_index("tp") % NC
    half = core if own else 1 - core
    for x in range(NX):
        for j in range(2):
            block = (2 * half + j) * 4 + (x + NY - at_y) % NY
            source = pl.ds(pl.multiple_of(block * TOK, TOK), TOK)
            picked_ref[pl.ds((2 * x + j) * TOK, TOK), :] = rows_ref[source, :]
    for y in range(NY):
        part = jnp.dot(
            picked_ref[...], weight_ref[y, :WEIGHT_ROWS], preferred_element_type=jnp.float32
        )
        width = part.shape[-1]
        part = part.reshape(NX, 2, TOK, width).astype(out_ref.dtype)
        for x in range(NX):
            for j in range(2):
                out_ref[x * NY + y, :, j * width : (j + 1) * width] = part[x, j]


def add(own_ref, added_ref, out_ref):
    for place in range(NY * NX):
        total = own_ref[place] + added_ref[place].astype(jnp.float32)
        out_ref[place] = total.astype(jnp.bfloat16)


def combine(parts_ref, out_ref):
    at_x = lax.axis_index("tp") // NC
    width = out_ref.shape[1]
    for y in range(NY):
        total = parts_ref[y].astype(jnp.float32)
        for x in range(1, NX):
            total += parts_ref[x * NY + y].astype(jnp.float32)
        total = total.astype(jnp.bfloat16)
        for j in range(2):
            block = 4 * j + (at_x + NY - y) % NY
            spot = pl.ds(pl.multiple_of(block * TOK, TOK), TOK)
            out_ref[spot, :] = total[:, j * width : (j + 1) * width]


def spread(weight_ref, q_ref, ids_ref, out_ref, held_ref, own_ref, in_sems, out_sems):
    width = weight_ref.shape[1]
    size = WEIGHT_ROWS // PIECES
    arrivals = []
    for piece in range(PIECES):
        part = pl.ds(piece * size, size)
        copy = pltpu.make_async_copy(weight_ref.at[part], held_ref.at[part], in_sems.at[piece])
        arrivals.append((part, [copy]))
    pieces = []
    for k in range(q_ref.shape[1] // width):
        target = held_ref.at[pl.ds(WEIGHT_ROWS + k * TOK, TOK)]
        source = q_ref.at[:, pl.ds(k * width, width)]
        pieces.append(pltpu.make_async_copy(source, target, in_sems.at[PIECES + k]))
    arrivals.append((pl.ds(WEIGHT_ROWS, SENT_ROWS - WEIGHT_ROWS), pieces))
    fetch = pltpu.make_async_copy(ids_ref, own_ref, in_sems.at[PIECES + 4])
    fetch.start()
    for _, copies in arrivals:
        for copy in copies:
            copy.start()
    leaving = []
    for index, (part, copies) in enumerate(arrivals):
        for copy in copies:
            copy.wait()
        if index == PIECES:
            fetch.wait()
            ids = own_ref[...]
            both = jnp.concatenate([ids & 127, ids >> 7, ids & 0, ids & 0], axis=1)
            both = jnp.broadcast_to(both.astype(jnp.float32), (SEG_ROWS, width))
            held_ref[WEIGHT_ROWS + QUERY_ROWS :] = both.astype(jnp.bfloat16)
        for y in range(NY):
            copy = pltpu.make_async_copy(
                held_ref.at[part], out_ref.at[y, part], out_sems.at[index, y]
            )
            copy.start()
            leaving.append(copy)
    for copy in leaving:
        copy.wait()


def body(queries, keys, values, segment_ids, out_weight):
    width = out_weight.shape[1]
    copies = pl.pallas_call(
        spread,
        out_shape=jax.ShapeDtypeStruct((NY, SENT_ROWS, width), jnp.bfloat16),
        in_specs=[ANY] * 3,
        out_specs=ANY,
        scratch_shapes=[
            pltpu.VMEM((SENT_ROWS, width), jnp.bfloat16),
            pltpu.VMEM((1, TOK), jnp.int32),
            pltpu.SemaphoreType.DMA((PIECES + 5,)),
            pltpu.SemaphoreType.DMA((PIECES + 1, NY)),
        ],
        compiler_params=pltpu.CompilerParams(vmem_limit_bytes=60 * 1024 * 1024),
    )(out_weight, queries, segment_ids.reshape(1, TOK))
    sent = lax.all_to_all(copies, "seq", 0, 0, axis_index_groups=Y_GROUPS, tiled=True)

    tag = jnp.concatenate([segment_ids % 128, segment_ids // 128])[None]
    tag = jnp.pad(tag, ((0, SEG_ROWS - 1), (0, 0))).astype(jnp.bfloat16)
    message = jnp.concatenate([keys, values, tag], axis=0)
    plane = lax.all_gather(message, "seq", axis_index_groups=Z_GROUPS)

    parts = pl.pallas_call(
        attend,
        out_shape=jax.ShapeDtypeStruct((NY, TOK, WIDE), jnp.bfloat16),
        in_specs=[VMEM] * 2,
        out_specs=VMEM,
        scratch_shapes=[pltpu.VMEM((CHUNKS, GROUP * TOK, CHUNK), jnp.float32)],
        compiler_params=pltpu.CompilerParams(vmem_limit_bytes=16 * 1024 * 1024),
        cost_estimate=pl.CostEstimate(
            flops=12 * GROUP * TOK * CHUNKS * CHUNK * HD,
            bytes_accessed=3 * 1024 * 1024,
            transcendentals=3 * GROUP * TOK * CHUNKS * CHUNK,
        ),
    )(sent, plane)
    parts = lax.all_to_all(parts, "seq", 0, 0, axis_index_groups=Y_GROUPS, tiled=True)
    attended = pl.pallas_call(
        merge,
        out_shape=jax.ShapeDtypeStruct((TOK, GROUP * HD), jnp.bfloat16),
        in_specs=[VMEM],
        out_specs=VMEM,
        compiler_params=pltpu.CompilerParams(vmem_limit_bytes=16 * 1024 * 1024),
    )(parts)

    rows = lax.all_gather(
        attended.astype(jnp.float16), "seq", axis_index_groups=Z_GROUPS, tiled=True
    ).astype(jnp.bfloat16)

    def projected(own, *operands):
        return pl.pallas_call(
            functools.partial(project, own),
            out_shape=jax.ShapeDtypeStruct(
                (NY * NX, TOK, 2 * width), jnp.float32 if own else jnp.bfloat16
            ),
            in_specs=[VMEM] * (1 + len(operands)),
            out_specs=VMEM,
            scratch_shapes=[pltpu.VMEM((PLANE // 2, GROUP * HD), jnp.bfloat16)],
            compiler_params=pltpu.CompilerParams(vmem_limit_bytes=16 * 1024 * 1024),
            cost_estimate=pl.CostEstimate(
                flops=PLANE * GROUP * HD * NY * width,
                bytes_accessed=6 * 1024 * 1024,
                transcendentals=0,
            ),
        )(rows, *operands)

    theirs = lax.ppermute(projected(False, sent), "tp", CORE_SWAP)
    sums = pl.pallas_call(
        add,
        out_shape=jax.ShapeDtypeStruct((NY * NX, TOK, 2 * width), jnp.bfloat16),
        in_specs=[VMEM] * 2,
        out_specs=VMEM,
        compiler_params=pltpu.CompilerParams(vmem_limit_bytes=16 * 1024 * 1024),
    )(projected(True, sent), theirs)
    parts = lax.all_to_all(
        sums, ("seq", "tp"), 0, 0, axis_index_groups=PLANE_GROUPS, tiled=True
    )
    return pl.pallas_call(
        combine,
        out_shape=jax.ShapeDtypeStruct((8 * TOK, width), jnp.bfloat16),
        in_specs=[VMEM],
        out_specs=VMEM,
        compiler_params=pltpu.CompilerParams(vmem_limit_bytes=16 * 1024 * 1024),
    )(parts)


def solution(mesh):
    return jax.shard_map(
        body,
        mesh=mesh,
        in_specs=(P("seq", "tp"), P("seq", "tp"), P("seq", "tp"), P("seq"), P("tp", "seq")),
        out_specs=P("tp", "seq"),
        check_vma=False,
    )
```

```python
import functools
import math

import jax
import jax.numpy as jnp
from jax import lax
from jax.experimental import pallas as pl
from jax.experimental.pallas import tpu as pltpu
from jax.sharding import PartitionSpec as P

HD = 128
GROUP = 8
TOK = 64
NY, NZ, NX, NC = 4, 16, 4, 2
CHUNK = 4 * TOK
CHUNKS = NZ // 4
HEADS_AT_ONCE = 4
PLANE = NZ * TOK
SEG_ROWS = 16
WEIGHT_ROWS = GROUP * HD
QUERY_ROWS = GROUP * TOK // 2
SENT_ROWS = WEIGHT_ROWS + QUERY_ROWS + SEG_ROWS
WIDE = GROUP * HD + 128
MASKED = -1e30
VMEM = pl.BlockSpec(memory_space=pltpu.VMEM)
ANY = pl.BlockSpec(memory_space=pl.ANY)

Y_GROUPS = [[y * NZ + z for y in range(NY)] for z in range(NZ)]
Z_GROUPS = [[y * NZ + z for z in range(NZ)] for y in range(NY)]
CORE_SWAP = [(t, t ^ 1) for t in range(NX * NC)]


def flat(y, z, x, c):
    return ((y * NZ + z) * NX + x) * NC + c


PLANE_GROUPS = [
    [flat(y, z, x, c) for x in range(NX) for y in range(NY)] for z in range(NZ) for c in range(NC)
]
def attend(sent_ref, plane_ref, out_ref, score_ref):
    at_y, at_z = lax.axis_index("seq") // NZ, lax.axis_index("seq") % NZ
    scale = math.log2(math.e) / math.sqrt(HD)
    count = HEADS_AT_ONCE * TOK
    rows = lax.broadcasted_iota(jnp.int32, (TOK, TOK), 0)
    cols = lax.broadcasted_iota(jnp.int32, (TOK, TOK), 1)
    lane = lax.broadcasted_iota(jnp.int32, (TOK, 128), 1)
    position = at_z * TOK + lax.broadcasted_iota(jnp.int32, (TOK, 1), 0)

    def ids_of(tile):
        pair = tile.astype(jnp.float32)[:1, : 2 * TOK]
        return pair[:, :TOK] + 128.0 * pair[:, TOK:]

    def part_of(i, start):
        return jnp.concatenate(
            [plane_ref[4 * i + j, start : start + TOK] for j in range(4)], axis=0
        )

    def key_ids(i):
        return jnp.concatenate(
            [ids_of(plane_ref[4 * i + j, 2 * TOK :]) for j in range(4)], axis=1
        )

    def band(ahead, chunks):
        y = at_y + ahead
        slot = (y + NY - at_z % NY) % NY
        own = ids_of(sent_ref[y, WEIGHT_ROWS + QUERY_ROWS :, :])
        own = jnp.sum(jnp.where(rows == cols, own, 0.0), axis=1, keepdims=True)
        keys = [part_of(i, 0) for i in chunks]
        values = [part_of(i, TOK) for i in chunks]
        keeps = []
        for i in chunks:
            keep = key_ids(i) == own
            if ahead == 0:
                at = i * CHUNK + lax.broadcasted_iota(jnp.int32, (TOK, CHUNK), 1)
                keep = keep & (at <= position)
            keeps.append(keep)
        marks = jnp.zeros((TOK, 128), jnp.float32)
        for first in range(0, GROUP, HEADS_AT_ONCE):
            heads = range(first, first + HEADS_AT_ONCE)
            queries = []
            for g in heads:
                row = WEIGHT_ROWS + g // 2 * TOK
                queries.append(sent_ref[y, row : row + TOK, g % 2 * HD : (g % 2 + 1) * HD])
            queries = jnp.concatenate(queries, axis=0)
            held = slice(first * TOK, first * TOK + count)
            best = jnp.full((count, HD), MASKED, jnp.float32)
            for n in range(len(chunks)):
                scores = lax.dot_general(
                    queries, keys[n], (((1,), (1,)), ((), ())), preferred_element_type=jnp.float32
                )
                scores = scores.reshape(HEADS_AT_ONCE, TOK, CHUNK)
                scores = jnp.where(keeps[n][None], scores, MASKED).reshape(count, CHUNK)
                score_ref[n, held] = scores
                best = jnp.maximum(best, jnp.maximum(scores[:, :HD], scores[:, HD:]))
            top = jnp.max(best, axis=1, keepdims=True) * scale
            total = jnp.zeros((count, HD), jnp.float32)
            mixed = jnp.zeros((count, HD), jnp.float32)
            for n in range(len(chunks)):
                weights = jnp.exp2(score_ref[n, held] * scale - top)
                total += weights[:, :HD] + weights[:, HD:]
                mixed += jnp.dot(
                    weights.astype(jnp.bfloat16), values[n], preferred_element_type=jnp.float32
                )
            total = jnp.sum(total, axis=1, keepdims=True)
            result = (mixed / total).astype(jnp.bfloat16)
            level = top + jnp.log2(total)
            high = level.astype(jnp.bfloat16).astype(jnp.float32)
            middle = (level - high).astype(jnp.bfloat16).astype(jnp.float32)
            for place, g in enumerate(heads):
                here = slice(place * TOK, (place + 1) * TOK)
                out_ref[slot, :, g * HD : (g + 1) * HD] = result[here]
                marks = jnp.where(lane == g, high[here], marks)
                marks = jnp.where(lane == GROUP + g, middle[here], marks)
                rest = level[here] - high[here] - middle[here]
                marks = jnp.where(lane == 2 * GROUP + g, rest, marks)
        out_ref[slot, :, GROUP * HD :] = marks.astype(jnp.bfloat16)

    low = at_z < NZ // 2
    cases = [
        (0, low, [0, 1]),
        (0, jnp.logical_not(low), [0, 1, 2, 3]),
        (1, at_y >= 0, [0, 1, 2, 3]),
        (2, low, [0, 1, 2, 3]),
        (2, jnp.logical_not(low), [1, 2, 3]),
        (3, at_z == 0, [3]),
    ]
    for ahead, when, chunks in cases:

        @pl.when((at_y + ahead < NY) & when)
        def _(ahead=ahead, chunks=chunks):
            band(ahead, chunks)

    for ahead in range(1, NY):
        unseen = at_y + ahead >= NY
        if ahead == 3:
            unseen = unseen | (at_z != 0)

        @pl.when(unseen)
        def _(ahead=ahead):
            slot = (at_y + ahead + NY - at_z % NY) % NY
            out_ref[slot, :, : GROUP * HD] = jnp.zeros((TOK, GROUP * HD), jnp.bfloat16)
            marks = jnp.where(lane < GROUP, MASKED, 0.0)
            out_ref[slot, :, GROUP * HD :] = marks.astype(jnp.bfloat16)


def merge(parts_ref, out_ref):
    levels = []
    for y in range(NY):
        marks = parts_ref[y, :, GROUP * HD :].astype(jnp.float32)
        levels.append(
            marks[:, :GROUP] + marks[:, GROUP : 2 * GROUP] + marks[:, 2 * GROUP : 3 * GROUP]
        )
    top = functools.reduce(jnp.maximum, levels)
    shares = [jnp.exp2(level - top) for level in levels]
    whole = sum(shares)
    shares = [share / whole for share in shares]
    for g in range(GROUP):
        across = slice(g * HD, (g + 1) * HD)
        total = jnp.zeros((TOK, HD), jnp.float32)
        for y in range(NY):
            total += shares[y][:, g : g + 1] * parts_ref[y, :, across].astype(jnp.float32)
        out_ref[:, across] = total.astype(jnp.bfloat16)


def project(own, rows_ref, weight_ref, *refs):
    out_ref, picked_ref = refs[-2:]
    at_y, core = lax.axis_index("seq") // NZ, lax.axis_index("tp") % NC
    half = core if own else 1 - core
    for x in range(NX):
        for j in range(2):
            block = (2 * half + j) * 4 + (x + NY - at_y) % NY
            source = pl.ds(pl.multiple_of(block * TOK, TOK), TOK)
            picked_ref[pl.ds((2 * x + j) * TOK, TOK), :] = rows_ref[source, :]
    for y in range(NY):
        part = jnp.dot(
            picked_ref[...], weight_ref[y, :WEIGHT_ROWS], preferred_element_type=jnp.float32
        )
        width = part.shape[-1]
        part = part.reshape(NX, 2, TOK, width).astype(out_ref.dtype)
        for x in range(NX):
            for j in range(2):
                out_ref[x * NY + y, :, j * width : (j + 1) * width] = part[x, j]


def add(own_ref, added_ref, out_ref):
    for place in range(NY * NX):
        total = own_ref[place] + added_ref[place].astype(jnp.float32)
        out_ref[place] = total.astype(jnp.bfloat16)


def combine(parts_ref, out_ref):
    at_x = lax.axis_index("tp") // NC
    width = out_ref.shape[1]
    for y in range(NY):
        total = parts_ref[y].astype(jnp.float32)
        for x in range(1, NX):
            total += parts_ref[x * NY + y].astype(jnp.float32)
        total = total.astype(jnp.bfloat16)
        for j in range(2):
            block = 4 * j + (at_x + NY - y) % NY
            spot = pl.ds(pl.multiple_of(block * TOK, TOK), TOK)
            out_ref[spot, :] = total[:, j * width : (j + 1) * width]


def spread(weight_ref, q_ref, ids_ref, out_ref, held_ref, own_ref, in_sems, out_sems):
    width = weight_ref.shape[1]
    half = WEIGHT_ROWS // 2
    arrivals = []
    for piece in range(2):
        part = pl.ds(piece * half, half)
        copy = pltpu.make_async_copy(weight_ref.at[part], held_ref.at[part], in_sems.at[piece])
        arrivals.append((part, [copy]))
    pieces = []
    for k in range(q_ref.shape[1] // width):
        target = held_ref.at[pl.ds(WEIGHT_ROWS + k * TOK, TOK)]
        source = q_ref.at[:, pl.ds(k * width, width)]
        pieces.append(pltpu.make_async_copy(source, target, in_sems.at[2 + k]))
    arrivals.append((pl.ds(WEIGHT_ROWS, SENT_ROWS - WEIGHT_ROWS), pieces))
    fetch = pltpu.make_async_copy(ids_ref, own_ref, in_sems.at[6])
    fetch.start()
    for _, copies in arrivals:
        for copy in copies:
            copy.start()
    leaving = []
    for index, (part, copies) in enumerate(arrivals):
        for copy in copies:
            copy.wait()
        if index == 2:
            fetch.wait()
            ids = own_ref[...]
            both = jnp.concatenate([ids & 127, ids >> 7, ids & 0, ids & 0], axis=1)
            both = jnp.broadcast_to(both.astype(jnp.float32), (SEG_ROWS, width))
            held_ref[WEIGHT_ROWS + QUERY_ROWS :] = both.astype(jnp.bfloat16)
        for y in range(NY):
            copy = pltpu.make_async_copy(
                held_ref.at[part], out_ref.at[y, part], out_sems.at[index, y]
            )
            copy.start()
            leaving.append(copy)
    for copy in leaving:
        copy.wait()


def body(queries, keys, values, segment_ids, out_weight):
    width = out_weight.shape[1]
    copies = pl.pallas_call(
        spread,
        out_shape=jax.ShapeDtypeStruct((NY, SENT_ROWS, width), jnp.bfloat16),
        in_specs=[ANY] * 3,
        out_specs=ANY,
        scratch_shapes=[
            pltpu.VMEM((SENT_ROWS, width), jnp.bfloat16),
            pltpu.VMEM((1, TOK), jnp.int32),
            pltpu.SemaphoreType.DMA((7,)),
            pltpu.SemaphoreType.DMA((3, NY)),
        ],
        compiler_params=pltpu.CompilerParams(vmem_limit_bytes=60 * 1024 * 1024),
    )(out_weight, queries, segment_ids.reshape(1, TOK))
    sent = lax.all_to_all(copies, "seq", 0, 0, axis_index_groups=Y_GROUPS, tiled=True)

    tag = jnp.concatenate([segment_ids % 128, segment_ids // 128])[None]
    tag = jnp.pad(tag, ((0, SEG_ROWS - 1), (0, 0))).astype(jnp.bfloat16)
    message = jnp.concatenate([keys, values, tag], axis=0)
    plane = lax.all_gather(message, "seq", axis_index_groups=Z_GROUPS)

    parts = pl.pallas_call(
        attend,
        out_shape=jax.ShapeDtypeStruct((NY, TOK, WIDE), jnp.bfloat16),
        in_specs=[VMEM] * 2,
        out_specs=VMEM,
        scratch_shapes=[pltpu.VMEM((CHUNKS, GROUP * TOK, CHUNK), jnp.float32)],
        compiler_params=pltpu.CompilerParams(vmem_limit_bytes=16 * 1024 * 1024),
        cost_estimate=pl.CostEstimate(
            flops=12 * GROUP * TOK * CHUNKS * CHUNK * HD,
            bytes_accessed=3 * 1024 * 1024,
            transcendentals=3 * GROUP * TOK * CHUNKS * CHUNK,
        ),
    )(sent, plane)
    parts = lax.all_to_all(parts, "seq", 0, 0, axis_index_groups=Y_GROUPS, tiled=True)
    attended = pl.pallas_call(
        merge,
        out_shape=jax.ShapeDtypeStruct((TOK, GROUP * HD), jnp.bfloat16),
        in_specs=[VMEM],
        out_specs=VMEM,
        compiler_params=pltpu.CompilerParams(vmem_limit_bytes=16 * 1024 * 1024),
    )(parts)

    rows = lax.all_gather(
        attended.astype(jnp.float16), "seq", axis_index_groups=Z_GROUPS, tiled=True
    ).astype(jnp.bfloat16)

    def projected(own, *operands):
        return pl.pallas_call(
            functools.partial(project, own),
            out_shape=jax.ShapeDtypeStruct(
                (NY * NX, TOK, 2 * width), jnp.float32 if own else jnp.bfloat16
            ),
            in_specs=[VMEM] * (1 + len(operands)),
            out_specs=VMEM,
            scratch_shapes=[pltpu.VMEM((PLANE // 2, GROUP * HD), jnp.bfloat16)],
            compiler_params=pltpu.CompilerParams(vmem_limit_bytes=16 * 1024 * 1024),
            cost_estimate=pl.CostEstimate(
                flops=PLANE * GROUP * HD * NY * width,
                bytes_accessed=6 * 1024 * 1024,
                transcendentals=0,
            ),
        )(rows, *operands)

    theirs = lax.ppermute(projected(False, sent), "tp", CORE_SWAP)
    sums = pl.pallas_call(
        add,
        out_shape=jax.ShapeDtypeStruct((NY * NX, TOK, 2 * width), jnp.bfloat16),
        in_specs=[VMEM] * 2,
        out_specs=VMEM,
        compiler_params=pltpu.CompilerParams(vmem_limit_bytes=16 * 1024 * 1024),
    )(projected(True, sent), theirs)
    parts = lax.all_to_all(
        sums, ("seq", "tp"), 0, 0, axis_index_groups=PLANE_GROUPS, tiled=True
    )
    return pl.pallas_call(
        combine,
        out_shape=jax.ShapeDtypeStruct((8 * TOK, width), jnp.bfloat16),
        in_specs=[VMEM],
        out_specs=VMEM,
        compiler_params=pltpu.CompilerParams(vmem_limit_bytes=16 * 1024 * 1024),
    )(parts)


def solution(mesh):
    return jax.shard_map(
        body,
        mesh=mesh,
        in_specs=(P("seq", "tp"), P("seq", "tp"), P("seq", "tp"), P("seq"), P("tp", "seq")),
        out_specs=P("tp", "seq"),
        check_vma=False,
    )
```
